32 devices in a mesh: groups: 2 (over x), ep: 16 (over z, y, core).
Axes of the slice: x: 2, y: 2, z: 4, core: 2. Of those that a mesh axis runs over, the one named last changes fastest.
Arguments:
- tokens: bfloat16 [256, 3072], P(('groups', 'ep')), parts along dimension 0, may hold values from -6 to 6
- cotangent: bfloat16 [256, 3072], P(('groups', 'ep')), parts along dimension 0, may hold values from -12 to 12
- routes: int32 [256, 4], P(('groups', 'ep')), parts along dimension 0, may hold values from 0 to 15, all different within a row; in each aligned block of 8 rows (0 to 7, 8 to 15, ...) at most 4 rows name the same one
- route_weights: bfloat16 [256, 4], P(('groups', 'ep')), parts along dimension 0, may hold values from 0.049804688 to 0.59765625
- w_gate: bfloat16 [43008, 3072], P('ep'), may hold values from -0.109375 to 0.109375
- w_up: bfloat16 [43008, 3072], P('ep'), may hold values from -0.109375 to 0.109375
- w_down: bfloat16 [43008, 3072], P('ep'), may hold values from -0.078125 to 0.078125
Outputs:
- token_grads: bfloat16 [256, 3072], P(('groups', 'ep')), parts along dimension 0
- grad_gate: bfloat16 [86016, 3072], P(('groups', 'ep')), parts along dimension 0
- grad_up: bfloat16 [86016, 3072], P(('groups', 'ep')), parts along dimension 0
- grad_down: bfloat16 [86016, 3072], P(('groups', 'ep')), parts along dimension 0
The draws below stay inside these ranges and needn't reach their ends.
There are 2 independent parts, one for each index of `groups`. The reference program is written for one: setup_inputs(seed, part) draws one part's arguments, and reference() takes and returns one part's arrays. A program takes and returns all parts, laid end to end along the dimension named above; an argument that names none is the same for every part. Nothing has to cross between parts.
Inputs may be any that keep to these rules, and one draw needn't show every extreme that they name: `routes`: each row names 4 different numbers. In each aligned block of 8 rows (the rows of one device) no number is named by more than 4 rows.
All inputs are finite; a program needn't handle non-finite values.
Results may differ from the reference program's by a relative error of at most 0.006.
Values may be sent and summed in bfloat16 or wider, within the bound.
A program may use at most 192 MiB of HBM per device.

```python
import math
import jax
import jax.numpy as jnp
import numpy as np
from jax import lax

D = 3072
FF = 5376
EXPERTS = 8
ROUTED = 16
TOP = 4
TOK_DEV = 8
CAP = 4
TOKENS = 128
N_EP = 16


def level_of(key, extent, cuts, smallest, high):
    def one(position, parts):
        heights = jax.random.uniform(jax.random.fold_in(jax.random.fold_in(key, 6), position), (parts,), jnp.float32, smallest / len(cuts), high / len(cuts))
        return jnp.repeat(jnp.exp(heights), extent[position] // parts).reshape((-1,) + (1,) * (len(extent) - position - 1))

    factor_of = one(*cuts[0])
    for cut in cuts[1:]:
        factor_of = factor_of * one(*cut)
    return factor_of


def deal_out(own_key, own, number, rows, number_of, top, most, lean):
    order = jax.random.permutation(own_key, number_of)
    heavy_load, usual = load_shares(number_of, rows * top, most, lean, True), load_shares(number_of, rows * top, most, lean, False)
    places = jnp.arange(number_of)

    def named(sizes, rotation):
        used = int((sizes > 0).sum())
        fixed = max(1, used // 4)
        passed = fixed + (places - fixed + rotation * (used - fixed)) % max(1, number_of - fixed)
        return jnp.zeros((number_of,), jnp.int32).at[order[jnp.where(places < fixed, places, passed)]].set(jnp.asarray(sizes, jnp.int32))

    sizes = jnp.where(number % 4 == 0, named(heavy_load, number // 4), named(usual, number - number // 4 - 1))
    mixed = jax.random.permutation(jax.random.fold_in(own, 3), number_of)
    giver, receiver = mixed[0:number_of // 2 * 2:2], mixed[1:number_of // 2 * 2:2]
    room = jnp.minimum(sizes[giver] - 1, most - sizes[receiver]) // 2
    room = jnp.where((giver == order[0]) | (receiver == order[0]) | (sizes[receiver] == 0), 0, jnp.maximum(room, 0))
    passed = jax.random.randint(jax.random.fold_in(own, 4), (number_of // 2,), 0, 1 << 20) % (room + 1)
    sizes = sizes.at[giver].add(-passed).at[receiver].add(passed)
    items = jnp.searchsorted(jnp.cumsum(sizes), jnp.arange(rows * top), side="right").astype(jnp.int32)
    grid = items.reshape(top, rows).T
    grid = grid[jax.random.permutation(jax.random.fold_in(own, 1), rows)]
    rotation = jax.random.randint(jax.random.fold_in(own, 2), (rows, 1), 0, top)
    return jnp.take_along_axis(grid, (jnp.arange(top)[None, :] + rotation) % top, axis=1)


def load_shares(count, total, bound, skew, full):
    loads = [(1 << 20) // math.isqrt(grade ** skew) + 1 for grade in range(1, count + 1)]
    largest = bound if full else min(bound, max(-(-total // count), total * loads[0] // sum(loads)))
    least = 1 if total - largest >= count - 1 else 0
    holding, spare = [largest] + [least] * (count - 1), total - largest - least * (count - 1)
    while spare > 0:
        candidates = [i for i in range(1, count) if holding[i] < largest] or [i for i in range(1, count) if holding[i] < bound]
        whole, remaining = sum([loads[i] for i in candidates]), spare
        for i in candidates:
            more = min(bound - holding[i], max(1, remaining * loads[i] // whole), spare)
            holding[i] = holding[i] + more
            spare = spare - more
    return np.array(holding)


def gaussian(own_key, shape, spread, limit, shards=(), kind=jnp.bfloat16):
    array = spread * jax.random.normal(own_key, shape, jnp.float32)
    if shards:
        array = array * level_of(own_key, shape, shards, -0.22, 0.18)
    return jnp.clip(array, -limit, limit).astype(kind)


def setup_inputs(seed: int = 0, part: int = 0) -> dict:
    arg_keys = jax.random.split(jax.random.key(seed), 8)
    own_keys = jax.random.split(jax.random.fold_in(arg_keys[7], part), 8)
    tokens = gaussian(own_keys[0], (TOKENS, D), 1.0, 6.0, ((0, 16),))
    cotangent = gaussian(own_keys[1], (TOKENS, D), 2.0, 12.0, ((0, 16),))
    routes_keys = jax.random.split(jax.random.fold_in(own_keys[2], 1), TOKENS // TOK_DEV)
    routes_turns = jax.random.permutation(jax.random.fold_in(own_keys[2], 3), TOKENS // TOK_DEV)
    routes = jax.vmap(lambda own, number: deal_out(jax.random.fold_in(own_keys[2], 2), own, number, TOK_DEV, ROUTED, TOP, CAP, 2))(routes_keys, routes_turns).reshape((TOKENS, TOP))
    route_weights = jnp.clip(jnp.exp(math.log(0.59765625) - 2.4849066 * jax.random.uniform(own_keys[3], (TOKENS, TOP), jnp.float32) ** level_of(own_keys[3], (TOKENS, TOP), ((0, 16),), -0.2, 0.2)), 0.049804688, 0.59765625).astype(jnp.bfloat16)
    w_gate = gaussian(arg_keys[4], (EXPERTS * FF, D), D ** -0.5, 0.109375, ((0, 16),))
    w_up = gaussian(arg_keys[5], (EXPERTS * FF, D), D ** -0.5, 0.109375, ((0, 16),))
    w_down = gaussian(arg_keys[6], (EXPERTS * FF, D), FF ** -0.5, 0.078125, ((0, 16),))
    return {"tokens": tokens, "cotangent": cotangent, "routes": routes, "route_weights": route_weights, "w_gate": w_gate, "w_up": w_up, "w_down": w_down}


def expert_math(row_tokens, row_cots, coefficient, gate_rows, up_rows, down_rows):
    gate_pre = jnp.dot(row_tokens, gate_rows.T, preferred_element_type=jnp.float32)
    up_pre = jnp.dot(row_tokens, up_rows.T, preferred_element_type=jnp.float32)
    sigmoid_gate = jax.nn.sigmoid(gate_pre)
    activated = gate_pre * sigmoid_gate
    hidden = (activated * up_pre).astype(jnp.bfloat16)
    out_grad = (coefficient[:, None] * row_cots.astype(jnp.float32)).astype(jnp.bfloat16)
    hidden_grad = jnp.dot(out_grad, down_rows.T, preferred_element_type=jnp.float32)
    grad_down = jnp.dot(hidden.T, out_grad, preferred_element_type=jnp.float32).astype(jnp.bfloat16)
    up_grad = (hidden_grad * activated).astype(jnp.bfloat16)
    gate_grad = (hidden_grad * up_pre * sigmoid_gate * (1.0 + gate_pre * (1.0 - sigmoid_gate))).astype(jnp.bfloat16)
    grad_up = jnp.dot(up_grad.T, row_tokens, preferred_element_type=jnp.float32).astype(jnp.bfloat16)
    grad_gate = jnp.dot(gate_grad.T, row_tokens, preferred_element_type=jnp.float32).astype(jnp.bfloat16)
    row_grads = jnp.dot(gate_grad, gate_rows, preferred_element_type=jnp.float32) + jnp.dot(up_grad, up_rows, preferred_element_type=jnp.float32)
    return (grad_gate, grad_up, grad_down), row_grads


def reference(tokens, cotangent, routes, route_weights, w_gate, w_up, w_down):
    total_rows = tokens.shape[0]
    slots_all = N_EP * CAP
    positions = jnp.arange(total_rows, dtype=jnp.int32)
    experts_iota = jnp.arange(EXPERTS, dtype=jnp.int32)
    matched = routes[:, :, None] == experts_iota[None, None, :]
    weight_table = jnp.sum(jnp.where(matched, route_weights.astype(jnp.float32)[:, :, None], jnp.float32(0.0)), axis=1)
    chosen = jnp.any(matched, axis=1)

    def per_expert(running, expert_index):
        picked = lax.dynamic_slice_in_dim(chosen, expert_index, 1, 1)[:, 0]
        sort_key = jnp.where(picked, 0, total_rows).astype(jnp.int32) + positions
        ordering = jnp.argsort(sort_key)[:slots_all].astype(jnp.int32)
        live_rows = picked[ordering]
        column = lax.dynamic_slice_in_dim(weight_table, expert_index, 1, 1)[:, 0]
        coefficient = jnp.where(live_rows, column[ordering], jnp.float32(0.0))
        first_row = (expert_index * FF).astype(jnp.int32)
        gate_rows = lax.dynamic_slice_in_dim(w_gate, first_row, FF, 0)
        up_rows = lax.dynamic_slice_in_dim(w_up, first_row, FF, 0)
        down_rows = lax.dynamic_slice_in_dim(w_down, first_row, FF, 0)
        gradients, row_grads = expert_math(tokens[ordering], cotangent[ordering], coefficient, gate_rows, up_rows, down_rows)
        running = running.at[ordering].add(row_grads)
        return running, gradients

    totals, stacked = lax.scan(per_expert, jnp.zeros((total_rows, D), jnp.float32), experts_iota)
    grad_gate = stacked[0].reshape(EXPERTS * FF, D)
    grad_up = stacked[1].reshape(EXPERTS * FF, D)
    grad_down = stacked[2].reshape(EXPERTS * FF, D)
    return (totals.astype(jnp.bfloat16), grad_gate, grad_up, grad_down)
```

```python
import functools
import jax
import jax.numpy as jnp
from jax import lax
from jax.experimental import pallas as pl
from jax.experimental.pallas import tpu as pltpu
from jax.sharding import PartitionSpec as P

EXPERTS = 8
CAP = 4
LANES = 128
CHUNK = 384
NCOL = 256
OUT_ROWS = 384
MESH = pl.DeviceIdType.MESH
F32 = jnp.float32
BF16 = jnp.bfloat16


def gather_blocks(blocks, send_sem, recv_sem):
    me = lax.axis_index("ep")
    z, y, c = me // 4, (me // 2) % 2, me % 2

    def place(zz, yy, cc):
        return (zz * 2 + yy) * 2 + cc

    up, down = place(z + 1, y, c), place(z - 1, y, c)
    across, sibling = place(z, 1 - y, c), place(z, y, 1 - c)

    def copy(kind, slot, target):
        return pltpu.make_async_remote_copy(
            src_ref=blocks.at[slot],
            dst_ref=blocks.at[slot],
            send_sem=send_sem.at[kind, slot],
            recv_sem=recv_sem.at[slot],
            device_id={"ep": target},
            device_id_type=MESH,
        )

    def landed(slot):
        copy(0, slot, sibling).wait_recv()

    def relay_from_below(slot):
        @pl.when(z < 3)
        def _():
            copy(1, slot, up).start()

    def relay_from_above(slot):
        @pl.when(z > 0)
        def _():
            copy(2, slot, down).start()

    def spread(slot):
        copy(3, slot, across).start()
        copy(0, slot, sibling).start()

    def crossed(zz):
        slot = place(zz, 1 - y, c)
        landed(slot)
        copy(0, slot, sibling).start()

    relay_from_below(me)
    relay_from_above(me)
    spread(me)
    for d in (1, 2, 3):

        @pl.when(z >= d)
        def _():
            slot = place(z - d, y, c)
            landed(slot)
            relay_from_below(slot)
            spread(slot)

        @pl.when(z + d <= 3)
        def _():
            slot = place(z + d, y, c)
            landed(slot)
            relay_from_above(slot)
            spread(slot)

        if d == 1:
            crossed(z)
        else:

            @pl.when(z >= d - 1)
            def _():
                crossed(z - (d - 1))

            @pl.when(z + d - 1 <= 3)
            def _():
                crossed(z + d - 1)

    @pl.when(z >= 3)
    def _():
        crossed(z - 3)

    @pl.when(z <= 0)
    def _():
        crossed(z + 3)

    for zz in range(4):
        for yy in range(2):
            landed(place(zz, yy, 1 - c))

    def drain():
        for zz in range(4):
            slot = place(zz, y, c)

            @pl.when((zz <= z) & (z < 3))
            def _():
                copy(1, slot, up).wait_send()

            @pl.when((zz >= z) & (z > 0))
            def _():
                copy(2, slot, down).wait_send()

            copy(3, slot, across).wait_send()
            copy(0, slot, sibling).wait_send()
            copy(0, place(zz, 1 - y, c), sibling).wait_send()

    return drain


def greet():
    me = lax.axis_index("ep")
    z = me // 4
    barrier = pltpu.get_barrier_semaphore()

    def hello(other):
        pl.semaphore_signal(barrier, inc=1, device_id={"ep": other}, device_id_type=MESH)

    hello(me + 1 - 2 * (me % 2))
    hello(me + 2 - 4 * ((me // 2) % 2))

    @pl.when(z > 0)
    def _():
        hello(me - 4)

    @pl.when(z < 3)
    def _():
        hello(me + 4)

    @pl.when((z > 0) & (z < 3))
    def _():
        pl.semaphore_wait(barrier, 4)

    @pl.when((z <= 0) | (z >= 3))
    def _():
        pl.semaphore_wait(barrier, 3)


def forward_kernel(
    tok_ref, cot_ref, routes_ref, rw_ref, wg_hbm, wu_hbm, wd_hbm,
    gu_ref, hid_ref, x_ref, og_ref, part_ref,
    w2, wd, blocks, xt, ogt, gut, wsem, send_sem, recv_sem,
):
    me = lax.axis_index("ep")
    expert = me // (lax.axis_size("ep") // EXPERTS)
    rows, width = tok_ref.shape
    hidden = wd.shape[0]
    parts = hidden // CHUNK
    n = blocks.shape[0]

    def weight_copies(i):
        at = pl.multiple_of(i * CHUNK, CHUNK)
        src = pl.ds(at, CHUNK)
        two = pl.multiple_of(i * 2 * CHUNK, CHUNK)
        return (
            pltpu.make_async_copy(wg_hbm.at[src], w2.at[pl.ds(two, CHUNK)], wsem.at[0, i]),
            pltpu.make_async_copy(wu_hbm.at[src], w2.at[pl.ds(two + CHUNK, CHUNK)], wsem.at[1, i]),
            pltpu.make_async_copy(wd_hbm.at[src], wd.at[src], wsem.at[2, i]),
        )

    for i in range(parts):
        for one in weight_copies(i):
            one.start()
    greet()

    lane = lax.broadcasted_iota(jnp.int32, (rows, LANES), 1)
    table = jnp.zeros((rows, LANES), F32)
    for k in range(routes_ref.shape[1]):
        table += jnp.where(lane == routes_ref[:, k : k + 1], rw_ref[:, k : k + 1].astype(F32), 0.0)
    own = jnp.concatenate([tok_ref[...].astype(F32), cot_ref[...].astype(F32)], axis=0)
    blocks[me, :, :width] = own.astype(BF16)
    blocks[me, :, width:] = jnp.concatenate([table, table], axis=0).astype(BF16)

    drain = gather_blocks(blocks, send_sem, recv_sem)

    for pair in range(n // 2):
        toks, ogs = [], []
        for b in (2 * pair, 2 * pair + 1):
            block = blocks[b].astype(F32)
            toks.append(block[:rows, :width])
            coef = jnp.sum(
                jnp.where(lane == expert, block[rows:, width:], 0.0), axis=1, keepdims=True
            )
            ogs.append(coef * block[rows:, :width])
        at = slice(2 * rows * pair, 2 * rows * (pair + 1))
        x_ref[at, :] = jnp.concatenate(toks, axis=0).astype(BF16)
        og_ref[at, :] = jnp.concatenate(ogs, axis=0).astype(BF16)
    for j in range(0, width, 512):
        xt[j : j + 512, :] = x_ref[:, j : j + 512].T
        ogt[j : j + 512, :] = og_ref[:, j : j + 512].T

    def forward(i, carry):
        for one in weight_copies(i):
            one.wait()
        at = pl.ds(pl.multiple_of(i * CHUNK, CHUNK), CHUNK)
        low = pl.multiple_of(i * 2 * CHUNK, CHUNK)
        both = jnp.dot(w2[pl.ds(low, 2 * CHUNK), :], xt[...], preferred_element_type=F32)
        gate, up = both[:CHUNK], both[CHUNK:]
        hgrad = jnp.dot(wd[at, :], ogt[...], preferred_element_type=F32)
        sig = 1.0 / (1.0 + jnp.exp(-gate))
        act = gate * sig
        hid_ref[at, :] = (act * up).astype(BF16)
        up_grad = (hgrad * act).astype(BF16)
        gate_grad = (hgrad * up * sig * (1.0 + gate * (1.0 - sig))).astype(BF16)
        gu_ref[pl.ds(low, CHUNK), :] = gate_grad
        gu_ref[pl.ds(low + CHUNK, CHUNK), :] = up_grad
        gut[:, pl.ds(low, CHUNK)] = gate_grad.T
        gut[:, pl.ds(low + CHUNK, CHUNK)] = up_grad.T
        return carry

    lax.fori_loop(0, parts, forward, 0)

    def back(j, carry):
        cols = pl.ds(pl.multiple_of(j * NCOL, NCOL), NCOL)
        part_ref[:, cols] = jnp.dot(gut[...], w2[:, cols], preferred_element_type=F32)
        return carry

    lax.fori_loop(0, width // NCOL, back, 0)
    drain()


def outer_kernel(gu_ref, hid_ref, x_ref, og_ref, gate_out, up_out, down_out):
    half = gate_out.shape[0]
    both = jnp.dot(gu_ref[...], x_ref[...], preferred_element_type=F32).astype(BF16)
    gate_out[...] = both[:half]
    up_out[...] = both[half:]
    down_out[...] = jnp.dot(hid_ref[...], og_ref[...], preferred_element_type=F32).astype(BF16)


def forward_call(tokens, cotangent, routes, route_weights, w_gate, w_up, w_down):
    n = lax.axis_size("ep")
    rows, width = tokens.shape
    hidden = w_gate.shape[0]
    total = n * rows
    parts = hidden // CHUNK
    vmem = pl.BlockSpec(memory_space=pltpu.VMEM)
    hbm = pl.BlockSpec(memory_space=pl.ANY)
    return pl.pallas_call(
        forward_kernel,
        out_shape=(
            jax.ShapeDtypeStruct((2 * hidden, total), BF16),
            jax.ShapeDtypeStruct((hidden, total), BF16),
            jax.ShapeDtypeStruct((total, width), BF16),
            jax.ShapeDtypeStruct((total, width), BF16),
            jax.ShapeDtypeStruct((total, width), F32),
        ),
        in_specs=[vmem] * 4 + [hbm] * 3,
        out_specs=(vmem,) * 5,
        scratch_shapes=[
            pltpu.VMEM((2 * hidden, width), BF16),
            pltpu.VMEM((hidden, width), BF16),
            pltpu.VMEM((n, 2 * rows, width + LANES), BF16),
            pltpu.VMEM((width, total), BF16),
            pltpu.VMEM((width, total), BF16),
            pltpu.VMEM((total, 2 * hidden), BF16),
            pltpu.SemaphoreType.DMA((3, parts)),
            pltpu.SemaphoreType.DMA((4, n)),
            pltpu.SemaphoreType.DMA((n,)),
        ],
        compiler_params=pltpu.CompilerParams(
            collective_id=0, has_side_effects=True, vmem_limit_bytes=63 * 1024 * 1024
        ),
        name="gather_forward",
    )(tokens, cotangent, routes, route_weights, w_gate, w_up, w_down)


def outer_call(gu, hid, x, og):
    hidden, total = hid.shape
    width = x.shape[1]
    whole = pl.BlockSpec((total, width), lambda i: (0, 0))
    out = pl.BlockSpec((OUT_ROWS, width), lambda i: (i, 0))
    shape = jax.ShapeDtypeStruct((hidden, width), BF16)
    return pl.pallas_call(
        outer_kernel,
        grid=(hidden // OUT_ROWS,),
        out_shape=(shape,) * 3,
        in_specs=[
            pl.BlockSpec((2 * OUT_ROWS, total), lambda i: (i, 0)),
            pl.BlockSpec((OUT_ROWS, total), lambda i: (i, 0)),
            whole,
            whole,
        ],
        out_specs=(out,) * 3,
        compiler_params=pltpu.CompilerParams(vmem_limit_bytes=48 * 1024 * 1024),
        cost_estimate=pl.CostEstimate(
            flops=6 * hidden * total * width,
            bytes_accessed=6 * hidden * width + 4 * total * width,
            transcendentals=0,
        ),
        name="weight_grads",
    )(gu, hid, x, og)


def fused_body(tokens, cotangent, routes, route_weights, w_gate, w_up, w_down):
    gu, hid, x, og, partial_grads = forward_call(
        tokens, cotangent, routes, route_weights, w_gate, w_up, w_down
    )
    token_grads = lax.psum_scatter(partial_grads, "ep", scatter_dimension=0, tiled=True)
    grad_gate, grad_up, grad_down = outer_call(gu, hid, x, og)
    return token_grads.astype(BF16), grad_gate, grad_up, grad_down


def route_table(routes, route_weights):
    experts_iota = jnp.arange(EXPERTS, dtype=jnp.int32)
    matched = routes[:, :, None] == experts_iota[None, None, :]
    weight_table = jnp.sum(
        jnp.where(matched, route_weights.astype(jnp.float32)[:, :, None], jnp.float32(0.0)), axis=1
    )
    return (jnp.any(matched, axis=1), weight_table)


def slot_matrix(chosen, capacity):
    rank_table = jnp.cumsum(chosen.astype(jnp.int32), axis=-1) - 1
    slot_iota = jnp.arange(capacity, dtype=jnp.int32)
    onehot = chosen[..., None, :] & (rank_table[..., None, :] == slot_iota[:, None])
    return onehot.astype(jnp.float32)


def slot_rank(chosen, capacity):
    rank_table = jnp.cumsum(chosen.astype(jnp.int32), axis=-1) - 1
    return jnp.clip(rank_table, 0, capacity - 1)


def expert_math(row_tokens, row_cots, coefficient, gate_rows, up_rows, down_rows):
    contract_last = (((1,), (1,)), ((), ()))
    contract_first = (((0,), (0,)), ((), ()))
    gate_pre = lax.dot_general(
        row_tokens, gate_rows, contract_last, preferred_element_type=jnp.float32
    )
    up_pre = lax.dot_general(row_tokens, up_rows, contract_last, preferred_element_type=jnp.float32)
    sigmoid_gate = jax.nn.sigmoid(gate_pre)
    activated = gate_pre * sigmoid_gate
    hidden = (activated * up_pre).astype(jnp.bfloat16)
    out_grad = (coefficient[:, None] * row_cots.astype(jnp.float32)).astype(jnp.bfloat16)
    hidden_grad = lax.dot_general(
        out_grad, down_rows, contract_last, preferred_element_type=jnp.float32
    )
    grad_down = lax.dot_general(
        hidden, out_grad, contract_first, preferred_element_type=jnp.float32
    ).astype(jnp.bfloat16)
    up_grad = (hidden_grad * activated).astype(jnp.bfloat16)
    gate_grad = (
        hidden_grad * up_pre * sigmoid_gate * (1.0 + gate_pre * (1.0 - sigmoid_gate))
    ).astype(jnp.bfloat16)
    grad_up = lax.dot_general(
        up_grad, row_tokens, contract_first, preferred_element_type=jnp.float32
    ).astype(jnp.bfloat16)
    grad_gate = lax.dot_general(
        gate_grad, row_tokens, contract_first, preferred_element_type=jnp.float32
    ).astype(jnp.bfloat16)
    row_grads = jnp.dot(gate_grad, gate_rows, preferred_element_type=jnp.float32) + jnp.dot(
        up_grad, up_rows, preferred_element_type=jnp.float32
    )
    return ((grad_gate, grad_up, grad_down), row_grads)


def body(tokens, cotangent, routes, route_weights, w_gate, w_up, w_down):
    cycle_size = lax.axis_size("ep")
    group_size = cycle_size // EXPERTS
    device_place = lax.axis_index("ep")
    expert_index = device_place // group_size
    local_rows, model_width = tokens.shape
    capacity = CAP
    slot_rows = cycle_size * capacity
    chosen, weight_table = route_table(routes, route_weights)
    all_tokens, all_cots, all_weights = (
        lax.all_gather(tokens, "ep", axis=0, tiled=True),
        lax.all_gather(cotangent, "ep", axis=0, tiled=True),
        lax.all_gather(weight_table.astype(jnp.bfloat16), "ep", axis=0, tiled=True),
    )
    column = (
        lax.dynamic_slice_in_dim(all_weights, expert_index, 1, 1)[:, 0]
        .astype(jnp.float32)
        .reshape(cycle_size, local_rows)
    )
    picked = column > 0.0
    block_slots = slot_matrix(picked, capacity)
    block_onehot = block_slots.astype(jnp.bfloat16)
    row_tokens = (
        jnp.einsum(
            "scj,sjd->scd",
            block_onehot,
            all_tokens.reshape(cycle_size, local_rows, model_width),
            preferred_element_type=jnp.float32,
        )
        .astype(jnp.bfloat16)
        .reshape(slot_rows, model_width)
    )
    row_cots = (
        jnp.einsum(
            "scj,sjd->scd",
            block_onehot,
            all_cots.reshape(cycle_size, local_rows, model_width),
            preferred_element_type=jnp.float32,
        )
        .astype(jnp.bfloat16)
        .reshape(slot_rows, model_width)
    )
    coefficient = jnp.sum(block_slots * column[:, None, :], axis=2).reshape(slot_rows)
    gradients, row_grads = expert_math(row_tokens, row_cots, coefficient, w_gate, w_up, w_down)
    block_rank = slot_rank(picked, capacity)
    looked_up = jnp.take_along_axis(
        row_grads.reshape(cycle_size, capacity, model_width), block_rank[:, :, None], axis=1
    )
    per_token = jnp.where(picked[:, :, None], looked_up, jnp.float32(0.0)).reshape(
        cycle_size * local_rows, model_width
    )
    token_grads = lax.psum_scatter(per_token, "ep", scatter_dimension=0, tiled=True)
    return (token_grads.astype(jnp.bfloat16), gradients[0], gradients[1], gradients[2])


def solution(mesh):
    placed = (
        P(("groups", "ep"), None),
        P(("groups", "ep"), None),
        P(("groups", "ep"), None),
        P(("groups", "ep"), None),
        P("ep", None),
        P("ep", None),
        P("ep", None),
    )
    return jax.shard_map(
        fused_body if mesh.shape["ep"] == 16 else body,
        mesh=mesh,
        in_specs=placed,
        out_specs=(
            P(("groups", "ep"), None),
            P(("groups", "ep"), None),
            P(("groups", "ep"), None),
            P(("groups", "ep"), None),
        ),
        check_vma=False,
    )
```

```python
import functools
import jax
import jax.numpy as jnp
from jax import lax
from jax.experimental import pallas as pl
from jax.experimental.pallas import tpu as pltpu
from jax.sharding import PartitionSpec as P

EXPERTS = 8
CAP = 4
LANES = 128
CHUNK = 384
HALF = 512
OUT_ROWS = 384
MESH = pl.DeviceIdType.MESH
F32 = jnp.float32
BF16 = jnp.bfloat16


def gather_blocks(blocks, send_sem, recv_sem):
    me = lax.axis_index("ep")
    z, y, c = me // 4, (me // 2) % 2, me % 2

    def place(zz, yy, cc):
        return (zz * 2 + yy) * 2 + cc

    up, down = place(z + 1, y, c), place(z - 1, y, c)
    across, sibling = place(z, 1 - y, c), place(z, y, 1 - c)

    def copy(kind, slot, target):
        return pltpu.make_async_remote_copy(
            src_ref=blocks.at[slot],
            dst_ref=blocks.at[slot],
            send_sem=send_sem.at[kind, slot],
            recv_sem=recv_sem.at[slot],
            device_id={"ep": target},
            device_id_type=MESH,
        )

    def landed(slot):
        copy(0, slot, sibling).wait_recv()

    def relay_from_below(slot):
        @pl.when(z < 3)
        def _():
            copy(1, slot, up).start()

    def relay_from_above(slot):
        @pl.when(z > 0)
        def _():
            copy(2, slot, down).start()

    def spread(slot):
        copy(3, slot, across).start()
        copy(0, slot, sibling).start()

    def crossed(zz):
        slot = place(zz, 1 - y, c)
        landed(slot)
        copy(0, slot, sibling).start()

    relay_from_below(me)
    relay_from_above(me)
    spread(me)
    for d in (1, 2, 3):

        @pl.when(z >= d)
        def _():
            slot = place(z - d, y, c)
            landed(slot)
            relay_from_below(slot)
            spread(slot)

        @pl.when(z + d <= 3)
        def _():
            slot = place(z + d, y, c)
            landed(slot)
            relay_from_above(slot)
            spread(slot)

        if d == 1:
            crossed(z)
        else:

            @pl.when(z >= d - 1)
            def _():
                crossed(z - (d - 1))

            @pl.when(z + d - 1 <= 3)
            def _():
                crossed(z + d - 1)

    @pl.when(z >= 3)
    def _():
        crossed(z - 3)

    @pl.when(z <= 0)
    def _():
        crossed(z + 3)

    for zz in range(4):
        for yy in range(2):
            landed(place(zz, yy, 1 - c))

    def drain():
        for zz in range(4):
            slot = place(zz, y, c)

            @pl.when((zz <= z) & (z < 3))
            def _():
                copy(1, slot, up).wait_send()

            @pl.when((zz >= z) & (z > 0))
            def _():
                copy(2, slot, down).wait_send()

            copy(3, slot, across).wait_send()
            copy(0, slot, sibling).wait_send()
            copy(0, place(zz, 1 - y, c), sibling).wait_send()

    return drain


def greet(n):
    me = lax.axis_index("ep")
    barrier = pltpu.get_barrier_semaphore()
    for k in range(1, n):
        pl.semaphore_signal(
            barrier, inc=1, device_id={"ep": (me + k) % n}, device_id_type=MESH
        )
    pl.semaphore_wait(barrier, n - 1)


def forward_kernel(
    tok_ref, cot_ref, routes_ref, rw_ref, wg_hbm, wu_hbm, wd_hbm,
    gu_ref, hid_ref, x_ref, og_ref, grads_ref,
    w2, wd, blocks, xt, ogt, gut, mine, pair_out, pair_in, out_blocks, in_blocks,
    wsem, send_sem, recv_sem, pair_send, pair_recv, out_sem, in_sem,
):
    me = lax.axis_index("ep")
    expert = me // (lax.axis_size("ep") // EXPERTS)
    rows, width = tok_ref.shape
    hidden = wd.shape[0]
    parts = hidden // CHUNK
    n = blocks.shape[0]

    def weight_copies(i):
        at = pl.multiple_of(i * CHUNK, CHUNK)
        src = pl.ds(at, CHUNK)
        two = pl.multiple_of(i * 2 * CHUNK, CHUNK)
        return (
            pltpu.make_async_copy(wg_hbm.at[src], w2.at[pl.ds(two, CHUNK)], wsem.at[0, i]),
            pltpu.make_async_copy(wu_hbm.at[src], w2.at[pl.ds(two + CHUNK, CHUNK)], wsem.at[1, i]),
            pltpu.make_async_copy(wd_hbm.at[src], wd.at[src], wsem.at[2, i]),
        )

    for i in range(parts):
        for one in weight_copies(i):
            one.start()
    greet(n)

    lane = lax.broadcasted_iota(jnp.int32, (rows, LANES), 1)
    number = lax.broadcasted_iota(jnp.int32, (LANES, rows), 0)
    by_expert = jnp.zeros((LANES, rows), F32)
    for k in range(routes_ref.shape[0]):
        by_expert += jnp.where(
            number == routes_ref[k : k + 1, :], rw_ref[k : k + 1, :].astype(F32), 0.0
        )
    same = lax.broadcasted_iota(jnp.int32, (rows, rows), 0) == lax.broadcasted_iota(
        jnp.int32, (rows, rows), 1
    )
    table = lax.dot_general(
        same.astype(BF16), by_expert.astype(BF16), (((1,), (1,)), ((), ())),
        preferred_element_type=F32,
    )
    own = jnp.concatenate([tok_ref[...].astype(F32), cot_ref[...].astype(F32)], axis=0)
    blocks[me, :, :width] = own.astype(BF16)
    blocks[me, :, width:] = jnp.concatenate([table, table], axis=0).astype(BF16)

    drain = gather_blocks(blocks, send_sem, recv_sem)

    for pair in range(n // 2):
        toks, ogs = [], []
        for b in (2 * pair, 2 * pair + 1):
            block = blocks[b].astype(F32)
            toks.append(block[:rows, :width])
            coef = jnp.sum(
                jnp.where(lane == expert, block[rows:, width:], 0.0), axis=1, keepdims=True
            )
            ogs.append(coef * block[rows:, :width])
        at = slice(2 * rows * pair, 2 * rows * (pair + 1))
        x_ref[at, :] = jnp.concatenate(toks, axis=0).astype(BF16)
        og_ref[at, :] = jnp.concatenate(ogs, axis=0).astype(BF16)
    for j in range(0, width, 512):
        xt[j : j + 512, :] = x_ref[:, j : j + 512].T
        ogt[j : j + 512, :] = og_ref[:, j : j + 512].T

    def forward(i, carry):
        for one in weight_copies(i):
            one.wait()
        at = pl.ds(pl.multiple_of(i * CHUNK, CHUNK), CHUNK)
        low = pl.multiple_of(i * 2 * CHUNK, CHUNK)
        both = jnp.dot(w2[pl.ds(low, 2 * CHUNK), :], xt[...], preferred_element_type=F32)
        gate, up = both[:CHUNK], both[CHUNK:]
        hgrad = jnp.dot(wd[at, :], ogt[...], preferred_element_type=F32)
        sig = 1.0 / (1.0 + jnp.exp(-gate))
        act = gate * sig
        hid_ref[at, :] = (act * up).astype(BF16)
        up_grad = (hgrad * act).astype(BF16)
        gate_grad = (hgrad * up * sig * (1.0 + gate * (1.0 - sig))).astype(BF16)
        gu_ref[pl.ds(low, CHUNK), :] = gate_grad
        gu_ref[pl.ds(low + CHUNK, CHUNK), :] = up_grad
        gut[:, pl.ds(low, CHUNK)] = gate_grad.T
        gut[:, pl.ds(low + CHUNK, CHUNK)] = up_grad.T
        return carry

    lax.fori_loop(0, parts, forward, 0)

    c = me % 2
    sibling = me + 1 - 2 * c
    steps = width // (2 * HALF)
    fold = HALF // 2

    def pair_copy(s):
        return pltpu.make_async_remote_copy(
            src_ref=pair_out.at[s],
            dst_ref=pair_in.at[s],
            send_sem=pair_send.at[s],
            recv_sem=pair_recv.at[s],
            device_id={"ep": sibling},
            device_id_type=MESH,
        )

    def owner_copy(s, owner, source):
        return pltpu.make_async_remote_copy(
            src_ref=out_blocks.at[s, owner],
            dst_ref=in_blocks.at[s, source],
            send_sem=out_sem.at[s, owner],
            recv_sem=in_sem.at[s, source],
            device_id={"ep": owner},
            device_id_type=MESH,
        )

    def columns(s, parity):
        start = pl.multiple_of((2 * s + parity) * HALF, HALF)
        return jnp.dot(gut[...], w2[:, pl.ds(start, HALF)], preferred_element_type=F32)

    def back(s, carry):
        pair_out[s] = columns(s, 1 - c)
        pair_copy(s).start()
        mine[...] = columns(s, c)
        pair_copy(s).wait_recv()
        for b in range(n):
            at = slice(b * rows, (b + 1) * rows)
            block = mine[at, :] + pair_in[s, at, :]
            out_blocks[s, b] = jnp.concatenate([block[:, :fold], block[:, fold:]], axis=0).astype(BF16)
        for k in range(1, n):
            owner_copy(s, (me + k) % n, me).start()
        in_blocks[s, me] = out_blocks[s, me]
        return carry

    lax.fori_loop(0, steps, back, 0)

    for s in range(steps):
        for k in range(1, n):
            owner_copy(s, me, (me + k) % n).wait_recv()
        for parity in range(2):
            total = in_blocks[s, parity].astype(F32)
            for q in range(1, n // 2):
                total += in_blocks[s, 2 * q + parity].astype(F32)
            start = (2 * s + parity) * HALF
            grads_ref[:, start : start + fold] = total[:rows].astype(BF16)
            grads_ref[:, start + fold : start + HALF] = total[rows:].astype(BF16)

    def finish(s, carry):
        pair_copy(s).wait_send()
        for k in range(1, n):
            owner_copy(s, (me + k) % n, me).wait_send()
        return carry

    lax.fori_loop(0, steps, finish, 0)
    drain()


def outer_kernel(gu_ref, hid_ref, x_ref, og_ref, gate_out, up_out, down_out):
    half = gate_out.shape[0]
    both = jnp.dot(gu_ref[...], x_ref[...], preferred_element_type=F32).astype(BF16)
    gate_out[...] = both[:half]
    up_out[...] = both[half:]
    down_out[...] = jnp.dot(hid_ref[...], og_ref[...], preferred_element_type=F32).astype(BF16)


def forward_call(tokens, cotangent, routes, route_weights, w_gate, w_up, w_down):
    n = lax.axis_size("ep")
    rows, width = tokens.shape
    hidden = w_gate.shape[0]
    total = n * rows
    parts = hidden // CHUNK
    steps = width // (2 * HALF)
    vmem = pl.BlockSpec(memory_space=pltpu.VMEM)
    hbm = pl.BlockSpec(memory_space=pl.ANY)
    return pl.pallas_call(
        forward_kernel,
        out_shape=(
            jax.ShapeDtypeStruct((2 * hidden, total), BF16),
            jax.ShapeDtypeStruct((hidden, total), BF16),
            jax.ShapeDtypeStruct((total, width), BF16),
            jax.ShapeDtypeStruct((total, width), BF16),
            jax.ShapeDtypeStruct((rows, width), BF16),
        ),
        in_specs=[vmem] * 4 + [hbm] * 3,
        out_specs=(vmem,) * 5,
        scratch_shapes=[
            pltpu.VMEM((2 * hidden, width), BF16),
            pltpu.VMEM((hidden, width), BF16),
            pltpu.VMEM((n, 2 * rows, width + LANES), BF16),
            pltpu.VMEM((width, total), BF16),
            pltpu.VMEM((width, total), BF16),
            pltpu.VMEM((total, 2 * hidden), BF16),
            pltpu.VMEM((total, HALF), F32),
            pltpu.VMEM((steps, total, HALF), F32),
            pltpu.VMEM((steps, total, HALF), F32),
            pltpu.VMEM((steps, n, 2 * rows, HALF // 2), BF16),
            pltpu.VMEM((steps, n, 2 * rows, HALF // 2), BF16),
            pltpu.SemaphoreType.DMA((3, parts)),
            pltpu.SemaphoreType.DMA((4, n)),
            pltpu.SemaphoreType.DMA((n,)),
            pltpu.SemaphoreType.DMA((steps,)),
            pltpu.SemaphoreType.DMA((steps,)),
            pltpu.SemaphoreType.DMA((steps, n)),
            pltpu.SemaphoreType.DMA((steps, n)),
        ],
        compiler_params=pltpu.CompilerParams(
            collective_id=0, has_side_effects=True, vmem_limit_bytes=63 * 1024 * 1024
        ),
        name="gather_forward",
    )(tokens, cotangent, routes.T, route_weights.T, w_gate, w_up, w_down)


def outer_call(gu, hid, x, og):
    hidden, total = hid.shape
    width = x.shape[1]
    whole = pl.BlockSpec((total, width), lambda i: (0, 0))
    out = pl.BlockSpec((OUT_ROWS, width), lambda i: (i, 0))
    shape = jax.ShapeDtypeStruct((hidden, width), BF16)
    return pl.pallas_call(
        outer_kernel,
        grid=(hidden // OUT_ROWS,),
        out_shape=(shape,) * 3,
        in_specs=[
            pl.BlockSpec((2 * OUT_ROWS, total), lambda i: (i, 0)),
            pl.BlockSpec((OUT_ROWS, total), lambda i: (i, 0)),
            whole,
            whole,
        ],
        out_specs=(out,) * 3,
        compiler_params=pltpu.CompilerParams(vmem_limit_bytes=63 * 1024 * 1024),
        cost_estimate=pl.CostEstimate(
            flops=6 * hidden * total * width,
            bytes_accessed=6 * hidden * width + 4 * total * width,
            transcendentals=0,
        ),
        name="weight_grads",
    )(gu, hid, x, og)


def fused_body(tokens, cotangent, routes, route_weights, w_gate, w_up, w_down):
    gu, hid, x, og, token_grads = forward_call(
        tokens, cotangent, routes, route_weights, w_gate, w_up, w_down
    )
    grad_gate, grad_up, grad_down = outer_call(gu, hid, x, og)
    return token_grads, grad_gate, grad_up, grad_down


def route_table(routes, route_weights):
    experts_iota = jnp.arange(EXPERTS, dtype=jnp.int32)
    matched = routes[:, :, None] == experts_iota[None, None, :]
    weight_table = jnp.sum(
        jnp.where(matched, route_weights.astype(jnp.float32)[:, :, None], jnp.float32(0.0)), axis=1
    )
    return (jnp.any(matched, axis=1), weight_table)


def slot_matrix(chosen, capacity):
    rank_table = jnp.cumsum(chosen.astype(jnp.int32), axis=-1) - 1
    slot_iota = jnp.arange(capacity, dtype=jnp.int32)
    onehot = chosen[..., None, :] & (rank_table[..., None, :] == slot_iota[:, None])
    return onehot.astype(jnp.float32)


def slot_rank(chosen, capacity):
    rank_table = jnp.cumsum(chosen.astype(jnp.int32), axis=-1) - 1
    return jnp.clip(rank_table, 0, capacity - 1)


def expert_math(row_tokens, row_cots, coefficient, gate_rows, up_rows, down_rows):
    contract_last = (((1,), (1,)), ((), ()))
    contract_first = (((0,), (0,)), ((), ()))
    gate_pre = lax.dot_general(
        row_tokens, gate_rows, contract_last, preferred_element_type=jnp.float32
    )
    up_pre = lax.dot_general(row_tokens, up_rows, contract_last, preferred_element_type=jnp.float32)
    sigmoid_gate = jax.nn.sigmoid(gate_pre)
    activated = gate_pre * sigmoid_gate
    hidden = (activated * up_pre).astype(jnp.bfloat16)
    out_grad = (coefficient[:, None] * row_cots.astype(jnp.float32)).astype(jnp.bfloat16)
    hidden_grad = lax.dot_general(
        out_grad, down_rows, contract_last, preferred_element_type=jnp.float32
    )
    grad_down = lax.dot_general(
        hidden, out_grad, contract_first, preferred_element_type=jnp.float32
    ).astype(jnp.bfloat16)
    up_grad = (hidden_grad * activated).astype(jnp.bfloat16)
    gate_grad = (
        hidden_grad * up_pre * sigmoid_gate * (1.0 + gate_pre * (1.0 - sigmoid_gate))
    ).astype(jnp.bfloat16)
    grad_up = lax.dot_general(
        up_grad, row_tokens, contract_first, preferred_element_type=jnp.float32
    ).astype(jnp.bfloat16)
    grad_gate = lax.dot_general(
        gate_grad, row_tokens, contract_first, preferred_element_type=jnp.float32
    ).astype(jnp.bfloat16)
    row_grads = jnp.dot(gate_grad, gate_rows, preferred_element_type=jnp.float32) + jnp.dot(
        up_grad, up_rows, preferred_element_type=jnp.float32
    )
    return ((grad_gate, grad_up, grad_down), row_grads)


def body(tokens, cotangent, routes, route_weights, w_gate, w_up, w_down):
    cycle_size = lax.axis_size("ep")
    group_size = cycle_size // EXPERTS
    device_place = lax.axis_index("ep")
    expert_index = device_place // group_size
    local_rows, model_width = tokens.shape
    capacity = CAP
    slot_rows = cycle_size * capacity
    chosen, weight_table = route_table(routes, route_weights)
    all_tokens, all_cots, all_weights = (
        lax.all_gather(tokens, "ep", axis=0, tiled=True),
        lax.all_gather(cotangent, "ep", axis=0, tiled=True),
        lax.all_gather(weight_table.astype(jnp.bfloat16), "ep", axis=0, tiled=True),
    )
    column = (
        lax.dynamic_slice_in_dim(all_weights, expert_index, 1, 1)[:, 0]
        .astype(jnp.float32)
        .reshape(cycle_size, local_rows)
    )
    picked = column > 0.0
    block_slots = slot_matrix(picked, capacity)
    block_onehot = block_slots.astype(jnp.bfloat16)
    row_tokens = (
        jnp.einsum(
            "scj,sjd->scd",
            block_onehot,
            all_tokens.reshape(cycle_size, local_rows, model_width),
            preferred_element_type=jnp.float32,
        )
        .astype(jnp.bfloat16)
        .reshape(slot_rows, model_width)
    )
    row_cots = (
        jnp.einsum(
            "scj,sjd->scd",
            block_onehot,
            all_cots.reshape(cycle_size, local_rows, model_width),
            preferred_element_type=jnp.float32,
        )
        .astype(jnp.bfloat16)
        .reshape(slot_rows, model_width)
    )
    coefficient = jnp.sum(block_slots * column[:, None, :], axis=2).reshape(slot_rows)
    gradients, row_grads = expert_math(row_tokens, row_cots, coefficient, w_gate, w_up, w_down)
    block_rank = slot_rank(picked, capacity)
    looked_up = jnp.take_along_axis(
        row_grads.reshape(cycle_size, capacity, model_width), block_rank[:, :, None], axis=1
    )
    per_token = jnp.where(picked[:, :, None], looked_up, jnp.float32(0.0)).reshape(
        cycle_size * local_rows, model_width
    )
    token_grads = lax.psum_scatter(per_token, "ep", scatter_dimension=0, tiled=True)
    return (token_grads.astype(jnp.bfloat16), gradients[0], gradients[1], gradients[2])


def solution(mesh):
    placed = (
        P(("groups", "ep"), None),
        P(("groups", "ep"), None),
        P(("groups", "ep"), None),
        P(("groups", "ep"), None),
        P("ep", None),
        P("ep", None),
        P("ep", None),
    )
    return jax.shard_map(
        fused_body if mesh.shape["ep"] == 16 else body,
        mesh=mesh,
        in_specs=placed,
        out_specs=(
            P(("groups", "ep"), None),
            P(("groups", "ep"), None),
            P(("groups", "ep"), None),
            P(("groups", "ep"), None),
        ),
        check_vma=False,
    )
```

```python
import functools
import jax
import jax.numpy as jnp
from jax import lax
from jax.experimental import pallas as pl
from jax.experimental.pallas import tpu as pltpu
from jax.sharding import PartitionSpec as P

EXPERTS = 8
CAP = 4
LANES = 128
CHUNK = 384
HALF = 512
OUT_COLS = 512
MESH = pl.DeviceIdType.MESH
F32 = jnp.float32
BF16 = jnp.bfloat16


def gather_blocks(blocks, send_sem, recv_sem):
    me = lax.axis_index("ep")
    z, y, c = me // 4, (me // 2) % 2, me % 2

    def place(zz, yy, cc):
        return (zz * 2 + yy) * 2 + cc

    across, sibling = place(z, 1 - y, c), place(z, y, 1 - c)

    def copy(kind, slot, target):
        return pltpu.make_async_remote_copy(
            src_ref=blocks.at[slot],
            dst_ref=blocks.at[slot],
            send_sem=send_sem.at[kind, slot],
            recv_sem=recv_sem.at[slot],
            device_id={"ep": target},
            device_id_type=MESH,
        )

    def landed(slot):
        copy(0, slot, across).wait_recv()

    def spread(slot):
        copy(4, slot, across).start()
        copy(0, slot, sibling).start()

    def begin():
        for d in (1, 2, 3):
            copy(d, me, place((z + d) % 4, y, c)).start()
        spread(me)

    def hop(d):
        slot = place((z + d) % 4, y, c)
        landed(slot)
        spread(slot)

    def cross(d):
        slot = place((z + d) % 4, 1 - y, c)
        landed(slot)
        copy(0, slot, sibling).start()

    def finish():
        for zz in range(4):
            for yy in range(2):
                landed(place(zz, yy, 1 - c))

    def drain():
        for d in (1, 2, 3):
            copy(d, me, place((z + d) % 4, y, c)).wait_send()
        for zz in range(4):
            copy(4, place(zz, y, c), across).wait_send()
            copy(0, place(zz, y, c), sibling).wait_send()
            copy(0, place(zz, 1 - y, c), sibling).wait_send()

    return begin, hop, cross, finish, drain


def greet(n):
    me = lax.axis_index("ep")
    barrier = pltpu.get_barrier_semaphore()
    for k in range(1, n):
        pl.semaphore_signal(
            barrier, inc=1, device_id={"ep": (me + k) % n}, device_id_type=MESH
        )
    pl.semaphore_wait(barrier, n - 1)


def forward_kernel(
    tok_ref, cot_ref, routes_ref, rw_ref, wg_hbm, wu_hbm, wd_hbm,
    gg_ref, ug_ref, hid_ref, x_ref, og_ref, grads_ref,
    w2, wd, tok_blocks, cot_blocks, pre, xt, ogt, gut, mine, pair_out, pair_in, out_blocks, in_blocks,
    summed, swapped, tab, slot_gut,
    wsem, tok_send, tok_recv, cot_send, cot_recv, pair_send, pair_recv, out_sem, in_sem, swap_sem,
):
    me = lax.axis_index("ep")
    expert = me // (lax.axis_size("ep") // EXPERTS)
    rows, width = tok_ref.shape
    hidden = wd.shape[0]
    parts = hidden // CHUNK
    n = tok_blocks.shape[0]
    half = width // 2

    def weight_copies(i):
        at = pl.multiple_of(i * CHUNK, CHUNK)
        src = pl.ds(at, CHUNK)
        two = pl.multiple_of(i * 2 * CHUNK, CHUNK)
        return (
            pltpu.make_async_copy(wg_hbm.at[src], w2.at[pl.ds(two, CHUNK)], wsem.at[0, i]),
            pltpu.make_async_copy(wu_hbm.at[src], w2.at[pl.ds(two + CHUNK, CHUNK)], wsem.at[1, i]),
            pltpu.make_async_copy(wd_hbm.at[src], wd.at[src], wsem.at[2, i]),
        )

    for i in range(parts):
        for one in weight_copies(i)[:2]:
            one.start()
    for i in range(parts):
        weight_copies(i)[2].start()
    greet(n)

    lane = lax.broadcasted_iota(jnp.int32, (rows, LANES), 1)
    number = lax.broadcasted_iota(jnp.int32, (LANES, rows), 0)
    by_expert = jnp.zeros((LANES, rows), F32)
    for k in range(routes_ref.shape[0]):
        by_expert += jnp.where(
            number == routes_ref[k : k + 1, :], rw_ref[k : k + 1, :].astype(F32), 0.0
        )
    same = lax.broadcasted_iota(jnp.int32, (rows, rows), 0) == lax.broadcasted_iota(
        jnp.int32, (rows, rows), 1
    )
    table = lax.dot_general(
        same.astype(BF16), by_expert.astype(BF16), (((1,), (1,)), ((), ())),
        preferred_element_type=F32,
    )
    tok = tok_ref[...].astype(F32)
    cot = cot_ref[...].astype(F32)
    tok_blocks[me] = jnp.concatenate([tok[:, :half], tok[:, half:]], axis=0).astype(BF16)
    cot_blocks[me, :, :half] = jnp.concatenate([cot[:, :half], cot[:, half:]], axis=0).astype(BF16)
    cot_blocks[me, :, half:] = jnp.concatenate([table, table], axis=0).astype(BF16)

    begin, hop, cross, finish, tok_drain = gather_blocks(tok_blocks, tok_send, tok_recv)
    cot_begin, cot_hop, cot_cross, cot_finish, cot_drain = gather_blocks(
        cot_blocks, cot_send, cot_recv
    )
    begin()
    cross(0)
    for d in (1, 2, 3):
        hop(d)
    cot_begin()
    for d in (1, 2, 3):
        cross(d)
    finish()

    def unfold(block):
        return jnp.concatenate([block[:rows, :half], block[rows:, :half]], axis=1)

    for pair in range(n // 2):
        at = slice(2 * rows * pair, 2 * rows * (pair + 1))
        toks = [unfold(tok_blocks[b].astype(F32)) for b in (2 * pair, 2 * pair + 1)]
        x_ref[at, :] = jnp.concatenate(toks, axis=0).astype(BF16)
    for j in range(0, width, 512):
        xt[j : j + 512, :] = x_ref[:, j : j + 512].T

    def pre_activations(i, carry):
        for one in weight_copies(i)[:2]:
            one.wait()
        both = pl.ds(pl.multiple_of(i * 2 * CHUNK, CHUNK), 2 * CHUNK)
        pre[both, :] = jnp.dot(w2[both, :], xt[...], preferred_element_type=F32)
        for d in (1, 2, 3):
            pl.when(i == 1)(functools.partial(cot_hop, d))
        for d in range(4):
            pl.when(i == 3)(functools.partial(cot_cross, d))
        return carry

    lax.fori_loop(0, parts, pre_activations, 0)
    cot_finish()

    for pair in range(n // 2):
        ogs, tables = [], []
        for b in (2 * pair, 2 * pair + 1):
            block = cot_blocks[b].astype(F32)
            coef = jnp.sum(
                jnp.where(lane == expert, block[:rows, half:], 0.0), axis=1, keepdims=True
            )
            ogs.append(coef * unfold(block))
            tables.append(block[:rows, half:])
        at = slice(2 * rows * pair, 2 * rows * (pair + 1))
        og_ref[at, :] = jnp.concatenate(ogs, axis=0).astype(BF16)
        tab[at, :] = jnp.concatenate(tables, axis=0).astype(BF16)
    for j in range(0, width, 512):
        ogt[j : j + 512, :] = og_ref[:, j : j + 512].T

    def forward(i, carry):
        weight_copies(i)[2].wait()
        at = pl.ds(pl.multiple_of(i * CHUNK, CHUNK), CHUNK)
        low = pl.multiple_of(i * 2 * CHUNK, CHUNK)
        high = pl.multiple_of(low + CHUNK, CHUNK)
        gate, up = pre[pl.ds(low, CHUNK), :], pre[pl.ds(high, CHUNK), :]
        hgrad = jnp.dot(wd[at, :], ogt[...], preferred_element_type=F32)
        sig = 1.0 / (1.0 + jnp.exp(-gate))
        act = gate * sig
        hid_ref[at, :] = (act * up).astype(BF16)
        up_grad = (hgrad * act).astype(BF16)
        gate_grad = (hgrad * up * sig * (1.0 + gate * (1.0 - sig))).astype(BF16)
        gg_ref[at, :] = gate_grad
        ug_ref[at, :] = up_grad
        gut[:, pl.ds(low, CHUNK)] = gate_grad.T
        gut[:, pl.ds(high, CHUNK)] = up_grad.T
        return carry

    lax.fori_loop(0, parts, forward, 0)

    c = me % 2
    sibling = me + 1 - 2 * c
    steps = width // (2 * HALF)
    fold = HALF // 2
    total_rows = n * rows

    def iota(shape, dim):
        return lax.broadcasted_iota(jnp.int32, shape, dim)

    pick = (iota((8, LANES), 1) == expert).astype(BF16)
    weight = lax.dot_general(
        pick, tab[...], (((1,), (1,)), ((), ())), preferred_element_type=F32
    )
    named = jnp.where(weight > 0.0, 1.0, 0.0)
    square = (total_rows, total_rows)
    before = (iota(square, 0) < iota(square, 1)) & (
        lax.div(iota(square, 0), rows) == lax.div(iota(square, 1), rows)
    )
    rank = jnp.dot(named.astype(BF16), before.astype(BF16), preferred_element_type=F32)
    wide = (n * CAP, total_rows)
    fits = (lax.div(iota(wide, 0), CAP) == lax.div(iota(wide, 1), rows)) & (
        rank[:1] == lax.rem(iota(wide, 0), CAP).astype(F32)
    )
    select = jnp.where(fits, named[:1], 0.0).astype(BF16)
    for j in range(0, 2 * hidden, 2 * CHUNK):
        cut = slice(j, j + 2 * CHUNK)
        slot_gut[:, cut] = jnp.dot(select, gut[:, cut], preferred_element_type=F32).astype(BF16)

    def pair_copy(s):
        return pltpu.make_async_remote_copy(
            src_ref=pair_out.at[s],
            dst_ref=pair_in.at[s],
            send_sem=pair_send.at[s],
            recv_sem=pair_recv.at[s],
            device_id={"ep": sibling},
            device_id_type=MESH,
        )

    chips = n // 2
    chip = me // 2

    def chip_copy(s, to, source):
        return pltpu.make_async_remote_copy(
            src_ref=out_blocks.at[s, to],
            dst_ref=in_blocks.at[s, source],
            send_sem=out_sem.at[s, to],
            recv_sem=in_sem.at[s, source],
            device_id={"ep": 2 * to + c},
            device_id_type=MESH,
        )

    def columns(s, parity):
        start = pl.multiple_of((2 * s + parity) * HALF, HALF)
        return jnp.dot(slot_gut[...], w2[:, pl.ds(start, HALF)], preferred_element_type=F32)

    def back(s, carry):
        pair_out[s] = columns(s, 1 - c)
        pair_copy(s).start()
        mine[...] = columns(s, c)
        pair_copy(s).wait_recv()
        for q in range(chips):
            at = slice(2 * q * CAP, 2 * (q + 1) * CAP)
            block = mine[at, :] + pair_in[s, at, :]
            out_blocks[s, q] = jnp.concatenate([block[:, :fold], block[:, fold:]], axis=0).astype(BF16)
        for k in range(1, chips):
            chip_copy(s, (chip + k) % chips, chip).start()
        in_blocks[s, chip] = out_blocks[s, chip]
        return carry

    lax.fori_loop(0, steps, back, 0)

    source = chips * 4 * CAP
    spot = iota((rows, source), 1)
    slot_of = lax.rem(spot, CAP).astype(F32)
    earlier = (iota((rows, rows), 0) > iota((rows, rows), 1)).astype(BF16)
    spread_out = (iota((LANES, source), 0) == lax.div(iota((LANES, source), 1), 4 * CAP)).astype(BF16)
    expand = []
    for owner in range(2):
        held = cot_blocks[2 * chip + owner].astype(F32)[:rows, half:]
        names = jnp.where(held > 0.0, 1.0, 0.0).astype(BF16)
        ranks = jnp.dot(earlier, names, preferred_element_type=F32).astype(BF16)
        names = jnp.dot(names, spread_out, preferred_element_type=F32)
        ranks = jnp.dot(ranks, spread_out, preferred_element_type=F32)
        for part in range(2):
            ours = lax.rem(lax.div(spot, CAP), 4) == 2 * part + owner
            expand.append(jnp.where(ours & (ranks == slot_of), names, 0.0))
    expand = jnp.concatenate(expand, axis=0).astype(BF16)

    for s in range(steps):
        for k in range(1, chips):
            chip_copy(s, chip, (chip + k) % chips).wait_recv()
        arrived = in_blocks[s].reshape(source, fold)
        total = jnp.dot(expand, arrived, preferred_element_type=F32)
        summed[0, s] = total[: 2 * rows].astype(BF16)
        summed[1, s] = total[2 * rows :].astype(BF16)

    swap = pltpu.make_async_remote_copy(
        src_ref=summed.at[1 - c],
        dst_ref=swapped,
        send_sem=swap_sem.at[0],
        recv_sem=swap_sem.at[1],
        device_id={"ep": sibling},
        device_id_type=MESH,
    )
    swap.start()

    def place_columns(s, parity, block):
        block = block.astype(F32)
        flat = jnp.concatenate([block[:rows], block[rows:]], axis=1)
        start = pl.multiple_of((2 * s + parity) * HALF, HALF)
        grads_ref[:, pl.ds(start, HALF)] = flat.astype(BF16)

    for s in range(steps):
        place_columns(s, c, summed[c, s])
    for s in range(steps):
        pair_copy(s).wait_send()
        for k in range(1, chips):
            chip_copy(s, (chip + k) % chips, chip).wait_send()
    swap.wait()
    for s in range(steps):
        place_columns(s, 1 - c, swapped[s])
    tok_drain()
    cot_drain()


def outer_kernel(gg_ref, ug_ref, hid_ref, x_ref, og_ref, gate_out, up_out, down_out):
    for left, right, out in (
        (gg_ref, x_ref, gate_out),
        (ug_ref, x_ref, up_out),
        (hid_ref, og_ref, down_out),
    ):
        out[...] = jnp.dot(left[...], right[...], preferred_element_type=F32).astype(BF16)


def forward_call(tokens, cotangent, routes, route_weights, w_gate, w_up, w_down):
    n = lax.axis_size("ep")
    rows, width = tokens.shape
    hidden = w_gate.shape[0]
    total = n * rows
    parts = hidden // CHUNK
    steps = width // (2 * HALF)
    vmem = pl.BlockSpec(memory_space=pltpu.VMEM)
    hbm = pl.BlockSpec(memory_space=pl.ANY)
    return pl.pallas_call(
        forward_kernel,
        out_shape=(
            jax.ShapeDtypeStruct((hidden, total), BF16),
            jax.ShapeDtypeStruct((hidden, total), BF16),
            jax.ShapeDtypeStruct((hidden, total), BF16),
            jax.ShapeDtypeStruct((total, width), BF16),
            jax.ShapeDtypeStruct((total, width), BF16),
            jax.ShapeDtypeStruct((rows, width), BF16),
        ),
        in_specs=[vmem] * 4 + [hbm] * 3,
        out_specs=(vmem,) * 6,
        scratch_shapes=[
            pltpu.VMEM((2 * hidden, width), BF16),
            pltpu.VMEM((hidden, width), BF16),
            pltpu.VMEM((n, 2 * rows, width // 2), BF16),
            pltpu.VMEM((n, 2 * rows, width // 2 + LANES), BF16),
            pltpu.VMEM((2 * hidden, total), F32),
            pltpu.VMEM((width, total), BF16),
            pltpu.VMEM((width, total), BF16),
            pltpu.VMEM((total, 2 * hidden), BF16),
            pltpu.VMEM((n * CAP, HALF), F32),
            pltpu.VMEM((steps, n * CAP, HALF), F32),
            pltpu.VMEM((steps, n * CAP, HALF), F32),
            pltpu.VMEM((steps, n // 2, 4 * CAP, HALF // 2), BF16),
            pltpu.VMEM((steps, n // 2, 4 * CAP, HALF // 2), BF16),
            pltpu.VMEM((2, steps, 2 * rows, HALF // 2), BF16),
            pltpu.VMEM((steps, 2 * rows, HALF // 2), BF16),
            pltpu.VMEM((total, LANES), BF16),
            pltpu.VMEM((n * CAP, 2 * hidden), BF16),
            pltpu.SemaphoreType.DMA((3, parts)),
            pltpu.SemaphoreType.DMA((5, n)),
            pltpu.SemaphoreType.DMA((n,)),
            pltpu.SemaphoreType.DMA((5, n)),
            pltpu.SemaphoreType.DMA((n,)),
            pltpu.SemaphoreType.DMA((steps,)),
            pltpu.SemaphoreType.DMA((steps,)),
            pltpu.SemaphoreType.DMA((steps, n // 2)),
            pltpu.SemaphoreType.DMA((steps, n // 2)),
            pltpu.SemaphoreType.DMA((2,)),
        ],
        compiler_params=pltpu.CompilerParams(
            collective_id=0, has_side_effects=True, vmem_limit_bytes=63 * 1024 * 1024
        ),
        name="gather_forward",
    )(tokens, cotangent, routes.T, route_weights.T, w_gate, w_up, w_down)


def outer_call(gg, ug, hid, x, og):
    hidden, total = hid.shape
    width = x.shape[1]
    rows = pl.BlockSpec((hidden, total), lambda i: (0, 0))
    narrow = pl.BlockSpec((total, OUT_COLS), lambda i: (0, i))
    out = pl.BlockSpec((hidden, OUT_COLS), lambda i: (0, i))
    shape = jax.ShapeDtypeStruct((hidden, width), BF16)
    return pl.pallas_call(
        outer_kernel,
        grid=(width // OUT_COLS,),
        out_shape=(shape,) * 3,
        in_specs=[rows, rows, rows, narrow, narrow],
        out_specs=(out,) * 3,
        compiler_params=pltpu.CompilerParams(vmem_limit_bytes=63 * 1024 * 1024),
        cost_estimate=pl.CostEstimate(
            flops=6 * hidden * total * width,
            bytes_accessed=6 * hidden * width + 4 * total * width,
            transcendentals=0,
        ),
        name="weight_grads",
    )(gg, ug, hid, x, og)


def fused_body(tokens, cotangent, routes, route_weights, w_gate, w_up, w_down):
    gg, ug, hid, x, og, token_grads = forward_call(
        tokens, cotangent, routes, route_weights, w_gate, w_up, w_down
    )
    grad_gate, grad_up, grad_down = outer_call(gg, ug, hid, x, og)
    return token_grads, grad_gate, grad_up, grad_down


def route_table(routes, route_weights):
    experts_iota = jnp.arange(EXPERTS, dtype=jnp.int32)
    matched = routes[:, :, None] == experts_iota[None, None, :]
    weight_table = jnp.sum(
        jnp.where(matched, route_weights.astype(jnp.float32)[:, :, None], jnp.float32(0.0)), axis=1
    )
    return (jnp.any(matched, axis=1), weight_table)


def slot_matrix(chosen, capacity):
    rank_table = jnp.cumsum(chosen.astype(jnp.int32), axis=-1) - 1
    slot_iota = jnp.arange(capacity, dtype=jnp.int32)
    onehot = chosen[..., None, :] & (rank_table[..., None, :] == slot_iota[:, None])
    return onehot.astype(jnp.float32)


def slot_rank(chosen, capacity):
    rank_table = jnp.cumsum(chosen.astype(jnp.int32), axis=-1) - 1
    return jnp.clip(rank_table, 0, capacity - 1)


def expert_math(row_tokens, row_cots, coefficient, gate_rows, up_rows, down_rows):
    contract_last = (((1,), (1,)), ((), ()))
    contract_first = (((0,), (0,)), ((), ()))
    gate_pre = lax.dot_general(
        row_tokens, gate_rows, contract_last, preferred_element_type=jnp.float32
    )
    up_pre = lax.dot_general(row_tokens, up_rows, contract_last, preferred_element_type=jnp.float32)
    sigmoid_gate = jax.nn.sigmoid(gate_pre)
    activated = gate_pre * sigmoid_gate
    hidden = (activated * up_pre).astype(jnp.bfloat16)
    out_grad = (coefficient[:, None] * row_cots.astype(jnp.float32)).astype(jnp.bfloat16)
    hidden_grad = lax.dot_general(
        out_grad, down_rows, contract_last, preferred_element_type=jnp.float32
    )
    grad_down = lax.dot_general(
        hidden, out_grad, contract_first, preferred_element_type=jnp.float32
    ).astype(jnp.bfloat16)
    up_grad = (hidden_grad * activated).astype(jnp.bfloat16)
    gate_grad = (
        hidden_grad * up_pre * sigmoid_gate * (1.0 + gate_pre * (1.0 - sigmoid_gate))
    ).astype(jnp.bfloat16)
    grad_up = lax.dot_general(
        up_grad, row_tokens, contract_first, preferred_element_type=jnp.float32
    ).astype(jnp.bfloat16)
    grad_gate = lax.dot_general(
        gate_grad, row_tokens, contract_first, preferred_element_type=jnp.float32
    ).astype(jnp.bfloat16)
    row_grads = jnp.dot(gate_grad, gate_rows, preferred_element_type=jnp.float32) + jnp.dot(
        up_grad, up_rows, preferred_element_type=jnp.float32
    )
    return ((grad_gate, grad_up, grad_down), row_grads)


def body(tokens, cotangent, routes, route_weights, w_gate, w_up, w_down):
    cycle_size = lax.axis_size("ep")
    group_size = cycle_size // EXPERTS
    device_place = lax.axis_index("ep")
    expert_index = device_place // group_size
    local_rows, model_width = tokens.shape
    capacity = CAP
    slot_rows = cycle_size * capacity
    chosen, weight_table = route_table(routes, route_weights)
    all_tokens, all_cots, all_weights = (
        lax.all_gather(tokens, "ep", axis=0, tiled=True),
        lax.all_gather(cotangent, "ep", axis=0, tiled=True),
        lax.all_gather(weight_table.astype(jnp.bfloat16), "ep", axis=0, tiled=True),
    )
    column = (
        lax.dynamic_slice_in_dim(all_weights, expert_index, 1, 1)[:, 0]
        .astype(jnp.float32)
        .reshape(cycle_size, local_rows)
    )
    picked = column > 0.0
    block_slots = slot_matrix(picked, capacity)
    block_onehot = block_slots.astype(jnp.bfloat16)
    row_tokens = (
        jnp.einsum(
            "scj,sjd->scd",
            block_onehot,
            all_tokens.reshape(cycle_size, local_rows, model_width),
            preferred_element_type=jnp.float32,
        )
        .astype(jnp.bfloat16)
        .reshape(slot_rows, model_width)
    )
    row_cots = (
        jnp.einsum(
            "scj,sjd->scd",
            block_onehot,
            all_cots.reshape(cycle_size, local_rows, model_width),
            preferred_element_type=jnp.float32,
        )
        .astype(jnp.bfloat16)
        .reshape(slot_rows, model_width)
    )
    coefficient = jnp.sum(block_slots * column[:, None, :], axis=2).reshape(slot_rows)
    gradients, row_grads = expert_math(row_tokens, row_cots, coefficient, w_gate, w_up, w_down)
    block_rank = slot_rank(picked, capacity)
    looked_up = jnp.take_along_axis(
        row_grads.reshape(cycle_size, capacity, model_width), block_rank[:, :, None], axis=1
    )
    per_token = jnp.where(picked[:, :, None], looked_up, jnp.float32(0.0)).reshape(
        cycle_size * local_rows, model_width
    )
    token_grads = lax.psum_scatter(per_token, "ep", scatter_dimension=0, tiled=True)
    return (token_grads.astype(jnp.bfloat16), gradients[0], gradients[1], gradients[2])


def solution(mesh):
    placed = (
        P(("groups", "ep"), None),
        P(("groups", "ep"), None),
        P(("groups", "ep"), None),
        P(("groups", "ep"), None),
        P("ep", None),
        P("ep", None),
        P("ep", None),
    )
    return jax.shard_map(
        fused_body if mesh.shape["ep"] == 16 else body,
        mesh=mesh,
        in_specs=placed,
        out_specs=(
            P(("groups", "ep"), None),
            P(("groups", "ep"), None),
            P(("groups", "ep"), None),
            P(("groups", "ep"), None),
        ),
        check_vma=False,
    )
```
